256 devices in a mesh: blk: 4 (over x), aux: 64 (over z, y, core).
Axes of the slice: x: 4, y: 4, z: 8, core: 2. Of those that a mesh axis runs over, the one named last changes fastest.
Arguments:
- integrals: float32 [192, 1536, 1536], P('aux', 'blk'), may hold values from -1.25 to 1.25
- orbitals: float32 [1536, 400], P('blk'), may hold values from -0.15625 to 0.15625
Outputs:
- exchange: float32 [1536, 1536], P(('blk', 'aux'))
The draws below stay inside these ranges and needn't reach their ends.
All inputs are finite; a program needn't handle non-finite values.
Results may differ from the reference program's by a relative error of at most 0.0001.
Values sent between devices are 32-bit elements; how exact they have to be, the bound alone decides.
A program may use at most 64 MiB of HBM per device.

```python
import jax
import jax.numpy as jnp
from jax import lax

OCC = 400
NBAS = 1536
NAUX = 192


def levels(key, extent, cuts, low, top_value):
    def one(dim, blocks):
        heights = jax.random.uniform(jax.random.fold_in(jax.random.fold_in(key, 6), dim), (blocks,), jnp.float32, low / len(cuts), top_value / len(cuts))
        return jnp.repeat(jnp.exp(heights), extent[dim] // blocks).reshape((-1,) + (1,) * (len(extent) - dim - 1))

    level = one(*cuts[0])
    for cut in cuts[1:]:
        level = level * one(*cut)
    return level


def bell_draw(stream_key, shape, scale, most, cuts=(), kind=jnp.bfloat16):
    values = jax.random.normal(stream_key, shape, jnp.float32) * scale
    if len(cuts) > 0:
        values = levels(stream_key, shape, cuts, -0.22, 0.18) * values
    return jnp.clip(values, min=-most, max=most).astype(kind)


def setup_inputs(seed: int = 0) -> dict:
    splits = jax.random.split(jax.random.key(seed), 3)
    integrals = bell_draw(splits[0], (NAUX, NBAS, NBAS), 0.085, 1.25, ((0, 64), (1, 4)), jnp.float32)
    orbitals = bell_draw(splits[1], (NBAS, OCC), NBAS ** -0.5, 0.15625, ((0, 4),), jnp.float32)
    return dict(integrals=integrals, orbitals=orbitals)


def reference(integrals, orbitals):
    def step(total, slab):
        half = jnp.dot(slab, orbitals, precision=lax.Precision.HIGHEST, preferred_element_type=jnp.float32)
        return total + jnp.dot(half, half.T, precision=lax.Precision.HIGHEST, preferred_element_type=jnp.float32), None
    start = jnp.zeros((integrals.shape[1], integrals.shape[1]), jnp.float32)
    total, unused = lax.scan(step, start, integrals)
    return total
```

```python
import jax
import jax.numpy as jnp
from jax import lax
from jax.experimental import pallas as pl
from jax.experimental.pallas import tpu as pltpu
from jax.sharding import PartitionSpec as P

MESH = pl.DeviceIdType.MESH
F32 = jnp.float32
BF16 = jnp.bfloat16
NP = 3
NB = 384
NL = 1536
OCC = 400
SL = 104
SLP = 112
K = NP * SLP
NBLK = 7
SETS = ((0, 1), (1, 2), (3, 4))


def split(v):
    hi = v.astype(BF16)
    return hi, (v - hi.astype(F32)).astype(BF16)


def nt(a, b):
    return lax.dot_general(a, b, (((1,), (1,)), ((), ())), preferred_element_type=F32)


def tn(a, b):
    return lax.dot_general(a, b, (((0,), (0,)), ((), ())), preferred_element_type=F32)


def kernel(
    ct_ref, i_ref, o_ref,
    i32, iperm, ihi, ilo, cf, chi, clo, h, xr, ohi, olo, xhi, xlo,
    g, gr, yr, zs, zr, fs, fr, onehot,
    isem, csend, crecv, fsend, frecv, hsend, hrecv, gsend, grecv, ysend, yrecv, zsend, zrecv, xsend, xrecv,
):
    x = lax.axis_index("blk")
    a = lax.axis_index("aux")
    z, y, c = a // 8, (a // 2) % 4, a % 2

    def dev(dx=0, dz=0, dy=0, dc=0):
        return ((x + dx) % 4, (((z + dz) % 8) * 4 + (y + dy) % 4) * 2 + (c + dc) % 2)

    def remote(src, dst, send, recv, to):
        return pltpu.make_async_remote_copy(
            src_ref=src, dst_ref=dst, send_sem=send, recv_sem=recv, device_id=to, device_id_type=MESH
        )

    loads = [pltpu.make_async_copy(i_ref.at[p], i32.at[p], isem.at[p]) for p in range(NP)]
    for load in loads:
        load.start()

    partners = [dict(dc=1)] + [dict(dx=d) for d in (1, 2, 3)] + [dict(dy=d) for d in (1, 2, 3)]
    partners += [dict(dz=d) for d in range(1, 8)]
    barrier = pltpu.get_barrier_semaphore()
    for partner in partners:
        pl.semaphore_signal(barrier, inc=1, device_id=dev(**partner), device_id_type=MESH)
    pl.semaphore_wait(barrier, len(partners))

    mine = pl.ds(pl.multiple_of(c * 200, 8), 200)
    theirs = pl.ds(pl.multiple_of((1 - c) * 200, 8), 200)
    sent = []
    for d in (1, 3, 2):
        copy = remote(ct_ref.at[mine], cf.at[x, mine], csend.at[d - 1], crecv.at[d - 1], dev(dx=d))
        copy.start()
        sent.append(copy)

    def prepare(p):
        loads[p].wait()
        for cc in range(2):
            for yy in range(4):
                for zz in range(8):
                    iperm[pl.ds(cc * 192 + yy * 48 + zz * 6, 6), :] = i32[p, pl.ds(zz * 48 + yy * 12 + cc * 6, 6), :]
        hi, lo = split(iperm[...])
        ihi[p] = hi
        ilo[p] = lo

    def forward(d):
        b = (x + 4 - d) % 4
        remote(ct_ref.at[mine], cf.at[b, mine], csend.at[d - 1], crecv.at[d - 1], dev(dx=d)).wait_recv()
        copy = remote(cf.at[b, mine], cf.at[b, mine], fsend.at[d - 1], frecv.at[d - 1], dev(dc=1))
        copy.start()
        sent.append(copy)

    for b in range(4):
        cf[b, pl.ds(OCC, 4 * SL - OCC), :] = jnp.zeros((4 * SL - OCC, NB), F32)
    cf[x, pl.ds(0, OCC), :] = ct_ref[...]
    rows = lax.broadcasted_iota(jnp.int32, (NB, NB), 0)
    cols = lax.broadcasted_iota(jnp.int32, (NB, NB), 1)
    place = ((cols // 6) % 2) * 192 + ((cols // 12) % 4) * 48 + (cols // 48) * 6 + cols % 6
    onehot[...] = jnp.where(rows == place, 1.0, 0.0).astype(BF16)
    prepare(0)
    prepare(1)
    forward(1)
    forward(3)
    prepare(2)
    forward(2)
    for d in (1, 3, 2):
        b = (x + 4 - d) % 4
        remote(cf.at[b, theirs], cf.at[b, theirs], fsend.at[d - 1], frecv.at[d - 1], dev(dc=1)).wait_recv()

    for b in range(4):
        v = jnp.concatenate(
            [cf[b, pl.ds(pl.multiple_of(((x + 2 + j) % 4) * SL, 8), SL), :] for j in range(4)], axis=0
        )
        hi, lo = split(v)
        chi[:, pl.ds(b * NB, NB)] = hi
        clo[:, pl.ds(b * NB, NB)] = lo

    extra_row = pl.multiple_of(jnp.where(c == 1, 3 * SL, 2 * SL), 8)
    extra_to = dev(dx=jnp.where(c == 1, 1, 3))

    def half_copies(p):
        plan = ((0, SL, dev(dx=1)), (1, 2 * SL, dev(dx=1)), (2, 3 * SL, dev(dx=3)), (3, 0, dev(dx=3)), (4, extra_row, extra_to))
        return [
            remote(h.at[p, pl.ds(row, SL)], xr.at[k, p], hsend.at[k, p], hrecv.at[k, p], to)
            for k, row, to in plan
        ]

    for p in range(NP):
        h[p] = nt(chi[...], ihi[p]) + nt(chi[...], ilo[p]) + nt(clo[...], ihi[p])
        for copy in half_copies(p):
            copy.start()

    pad = jnp.zeros((SLP - SL, NB), F32)
    for p in range(NP):
        for j in range(4):
            hi, lo = split(jnp.concatenate([h[p, pl.ds(j * SL, SL), :], pad], axis=0))
            ohi[pl.ds(j * K + p * SLP, SLP), :] = hi
            olo[pl.ds(j * K + p * SLP, SLP), :] = lo

    def pair_start(s):
        k0, nk = SETS[s]
        remote(
            g.at[pl.ds(k0, nk), pl.ds(pl.multiple_of((1 - c) * 192, 8), 192)], gr.at[pl.ds(k0, nk)],
            gsend.at[s], grecv.at[s], dev(dc=1),
        ).start()

    def pair_wait(s):
        k0, nk = SETS[s]
        remote(
            g.at[pl.ds(k0, nk), pl.ds(pl.multiple_of((1 - c) * 192, 8), 192)], gr.at[pl.ds(k0, nk)],
            gsend.at[s], grecv.at[s], dev(dc=1),
        ).wait()
        own = pl.ds(pl.multiple_of(c * 192, 8), 192)
        for k in range(k0, k0 + nk):
            g[k, own, :] += gr[k]

    def y_copies(s):
        k0, nk = SETS[s]
        return [
            remote(
                g.at[pl.ds(k0, nk), pl.ds(pl.multiple_of(c * 192 + ((y + d) % 4) * 48, 8), 48)],
                yr.at[d - 1, pl.ds(k0, nk)], ysend.at[d - 1, s], yrecv.at[d - 1, s], dev(dy=d),
            )
            for d in (1, 3, 2)
        ]

    def z_copies(s):
        k0, nk = SETS[s]
        return [
            remote(
                zs.at[(z + d) % 8, pl.ds(k0, nk)], zr.at[d - 1, pl.ds(k0, nk)],
                zsend.at[d - 1, s], zrecv.at[d - 1, s], dev(dz=d),
            )
            for d in (4, 3, 5, 2, 6, 1, 7)
        ]

    def y_start(s):
        for copy in y_copies(s):
            copy.start()

    def y_finish(s):
        for copy in y_copies(s):
            copy.wait_recv()
        k0, nk = SETS[s]
        for k in range(k0, k0 + nk):
            v = g[k, pl.ds(pl.multiple_of(c * 192 + y * 48, 8), 48), :] + yr[0, k] + yr[1, k] + yr[2, k]
            for zz in range(8):
                zs[zz, k] = v[zz * 6 : zz * 6 + 6, :]
        for copy in z_copies(s):
            copy.start()

    def gram(ahi, alo, bhi, blo):
        return tn(ahi, bhi) + tn(ahi, blo) + tn(alo, bhi)

    def take(p):
        copies = half_copies(p)
        for k, copy in enumerate(copies):
            copy.wait_recv()
            hi, lo = split(jnp.concatenate([xr[k, p], pad], axis=0))
            xhi[pl.ds(k * K + p * SLP, SLP), :] = hi
            xlo[pl.ds(k * K + p * SLP, SLP), :] = lo

    def own(j, n):
        return ohi[pl.ds(j * K, n * K), :], olo[pl.ds(j * K, n * K), :]

    def got(j, n):
        return xhi[pl.ds(j * K, n * K), :], xlo[pl.ds(j * K, n * K), :]

    g[0] = gram(*own(0, 4), *own(0, 4))
    pair_start(0)
    take(0)
    pair_wait(0)
    y_start(0)
    take(1)
    y_finish(0)
    take(2)

    g[1] = gram(*own(0, 2), *got(2, 2))
    g[2] = gram(*own(1, 1), *got(1, 1))
    extra_k = pl.ds(pl.multiple_of(jnp.where(c == 1, 2 * K, 3 * K), 16), K)
    extra_blk = jnp.where(c == 1, 2, 1)
    g[extra_blk] += gram(ohi[extra_k, :], olo[extra_k, :], *got(4, 1))
    pair_start(1)
    g[6] = gram(*got(0, 2), *got(2, 2))
    g[3] = g[1].T
    g[4] = g[6].T
    g[5] = g[2].T
    pair_start(2)
    pair_wait(1)
    y_start(1)
    pair_wait(2)
    y_start(2)
    y_finish(1)
    y_finish(2)
    for s in range(len(SETS)):
        for copy in z_copies(s):
            copy.wait_recv()

    def total(k):
        v = zs[z, k]
        for d in range(7):
            v = v + zr[d, k]
        return v

    for k in range(4):
        fs[k] = total(3 + k)
    x_copies = [
        remote(fs.at[pl.ds(2 * k, 2)], fr.at[pl.ds(2 * k, 2)], xsend.at[k], xrecv.at[k], dev(dx=d))
        for k, d in ((0, 1), (1, 3))
    ]
    for copy in x_copies:
        copy.start()
    mid, right, left = total(0), total(1), total(2)
    for copy in x_copies:
        copy.wait_recv()
    parts = (mid, right + fr[2], fr[1] + fr[3], left + fr[0])
    for d, v in enumerate(parts):
        hi, rest = v.astype(BF16), v
        out = jnp.zeros((6, NB), F32)
        for _ in range(3):
            out = out + jnp.dot(hi, onehot[...], preferred_element_type=F32)
            rest = rest - hi.astype(F32)
            hi = rest.astype(BF16)
        o_ref[:, pl.ds(pl.multiple_of(((x + d) % 4) * NB, 128), NB)] = out

    for copy in sent:
        copy.wait_send()
    for p in range(NP):
        for copy in half_copies(p):
            copy.wait_send()
    for s in range(len(SETS)):
        for copy in y_copies(s) + z_copies(s):
            copy.wait_send()
    for copy in x_copies:
        copy.wait_send()


def per_device(integrals, orbitals):
    dma = pltpu.SemaphoreType.DMA
    return pl.pallas_call(
        kernel,
        out_shape=jax.ShapeDtypeStruct((6, NL), F32),
        in_specs=[pl.BlockSpec(memory_space=pltpu.VMEM), pl.BlockSpec(memory_space=pl.ANY)],
        out_specs=pl.BlockSpec(memory_space=pltpu.VMEM),
        scratch_shapes=[
            pltpu.VMEM((NP, NB, NL), F32),
            pltpu.VMEM((NB, NL), F32),
            pltpu.VMEM((NP, NB, NL), BF16),
            pltpu.VMEM((NP, NB, NL), BF16),
            pltpu.VMEM((4, 4 * SL, NB), F32),
            pltpu.VMEM((4 * SL, NL), BF16),
            pltpu.VMEM((4 * SL, NL), BF16),
            pltpu.VMEM((NP, 4 * SL, NB), F32),
            pltpu.VMEM((5, NP, SL, NB), F32),
            pltpu.VMEM((4 * K, NB), BF16),
            pltpu.VMEM((4 * K, NB), BF16),
            pltpu.VMEM((5 * K, NB), BF16),
            pltpu.VMEM((5 * K, NB), BF16),
            pltpu.VMEM((NBLK, NB, NB), F32),
            pltpu.VMEM((NBLK, NB // 2, NB), F32),
            pltpu.VMEM((3, NBLK, 48, NB), F32),
            pltpu.VMEM((8, NBLK, 6, NB), F32),
            pltpu.VMEM((7, NBLK, 6, NB), F32),
            pltpu.VMEM((4, 6, NB), F32),
            pltpu.VMEM((4, 6, NB), F32),
            pltpu.VMEM((NB, NB), BF16),
            dma((NP,)),
            dma((3,)), dma((3,)), dma((3,)), dma((3,)),
            dma((5, NP)), dma((5, NP)),
            dma((3,)), dma((3,)),
            dma((3, 3)), dma((3, 3)),
            dma((7, 3)), dma((7, 3)),
            dma((2,)), dma((2,)),
        ],
        compiler_params=pltpu.CompilerParams(
            collective_id=0, has_side_effects=True, vmem_limit_bytes=56 << 20
        ),
    )(orbitals.T, integrals)


def solution(mesh):
    return jax.shard_map(
        per_device,
        mesh=mesh,
        in_specs=(P("aux", "blk", None), P("blk", None)),
        out_specs=P(("blk", "aux"), None),
        check_vma=False,
    )
```

```python
import jax
import jax.numpy as jnp
from jax import lax
from jax.experimental import pallas as pl
from jax.experimental.pallas import tpu as pltpu
from jax.sharding import PartitionSpec as P

MESH = pl.DeviceIdType.MESH
F32 = jnp.float32
BF16 = jnp.bfloat16
NP = 3
NB = 384
NL = 1536
OCC = 400
SL = 104
SLP = 112
K = NP * SLP
T = 128
CUT = 56


def tile_sets():
    sets = [[(0, 0, r, c) for r in range(3) for c in range(3)]]
    for t in range(3):
        left = [(0, -1, r, t) for r in range(3)] + [(-1, 0, t, c) for c in range(3)]
        rest = [(0, 1, r, t) for r in range(3)] + [(1, 0, t, c) for c in range(3)]
        for d in (-1, 1):
            rest += [(d, -d, t, c) for c in range(t + 1)] + [(d, -d, r, t) for r in range(t)]
        sets += [left, rest] if t == 2 else [left + rest]
    return sets


SETS = tile_sets()
SLOT = {tile: i for i, tile in enumerate(sum(SETS, []))}
ENDS = [sum(len(s) for s in SETS[: i + 1]) for i in range(len(SETS))]
SPANS = [(e - len(s), len(s)) for s, e in zip(SETS, ENDS)]
GSPANS = {0: (0, 2), 1: (2, 3), 2: (5, 5), 4: (10, 6)}


def split(v):
    hi = v.astype(BF16)
    return hi, (v - hi.astype(F32)).astype(BF16)


def nt(a, b):
    return lax.dot_general(a, b, (((1,), (1,)), ((), ())), preferred_element_type=F32)


def tn(a, b):
    return lax.dot_general(a, b, (((0,), (0,)), ((), ())), preferred_element_type=F32)


def gram(a, b):
    return tn(a[0], b[0]) + tn(a[0], b[1]) + tn(a[1], b[0])


def kernel(
    ct_ref, i_ref, o_ref,
    i32, ihi, ilo, cf, chi, clo, h, xr, ohi, olo, xhi, xlo,
    g, gr, yr, ybuf, zs, zr, f, fs, fr, onehot,
    relay, isem, csend, crecv, fsend, frecv, hsend, hrecv, gsend, grecv, ysend, yrecv, zsend, zrecv, xsend, xrecv,
):
    x = lax.axis_index("blk")
    a = lax.axis_index("aux")
    z, y, c = a // 8, (a // 2) % 4, a % 2
    started = []

    def dev(dx=0, dz=0, dy=0, dc=0):
        return ((x + dx) % 4, (((z + dz) % 8) * 4 + (y + dy) % 4) * 2 + (c + dc) % 2)

    def remote(src, dst, send, recv, to):
        return pltpu.make_async_remote_copy(
            src_ref=src, dst_ref=dst, send_sem=send, recv_sem=recv, device_id=to, device_id_type=MESH
        )

    def start(copy):
        copy.start()
        started.append(copy)

    def arrive(copy):
        copy.wait_recv()

    def at(row):
        return pl.multiple_of(row, 8)

    def work():
        loads = [
            pltpu.make_async_copy(i_ref.at[p, :, pl.ds(q * T, T)], i32.at[p, q], isem.at[p, q])
            for p in range(NP) for q in range(12)
        ]
        for load in loads:
            load.start()

        partners = [dict(dx=2), dict(dx=1), dict(dx=3), dict(dz=1), dict(dz=7), dict(dy=1), dict(dy=3), dict(dc=1)]
        barrier = pltpu.get_barrier_semaphore()
        for partner in partners:
            pl.semaphore_signal(barrier, inc=1, device_id=dev(**partner), device_id_type=MESH)
        cf[x, pl.ds(0, OCC), :] = ct_ref[...]
        cf[x, pl.ds(OCC, 4 * SL - OCC), :] = jnp.zeros((4 * SL - OCC, NB), F32)
        pl.semaphore_wait(barrier, len(partners))

        gather = {}

        def area(b, n, core, r0=0, nr=SL):
            return cf.at[b, pl.ds(at((2 * core + n) * SL + r0), nr)]

        def fetch(n, i, b, come, to, r0=0, nr=SL):
            mine, here = area(b, n, c, r0, nr), area(come, n, c, r0, nr)
            sems = csend.at[n, i], crecv.at[n, i]
            gather[n, i] = come, r0, nr, remote(here, here, *sems, to)
            start(remote(mine, mine, *sems, to))

        def block_at(dx):
            return (x + dx) % 4

        for n in range(2):
            fetch(n, 0, x, block_at(3), dev(dx=1))
            fetch(n, 1, x, block_at(1), dev(dx=3))
            if n == 0:
                fetch(n, 2, x, block_at(2), dev(dx=2))

        def tell(i, **to):
            pl.semaphore_signal(relay.at[i], inc=1, device_id=dev(**to), device_id_type=MESH)

        tell(0, dy=1)
        tell(1, dz=1)
        tell(2, dz=7)

        def forward(n, i):
            b, r0, nr, copy = gather[n, i]
            arrive(copy)
            mine, there = area(b, n, c, r0, nr), area(b, n, 1 - c, r0, nr)
            sems = fsend.at[n, i], frecv.at[n, i]
            gather[n, i] = remote(there, there, *sems, dev(dc=1))
            if n == 1 and i == 0:
                fetch(n, 2, b, block_at(2), dev(dx=1), 0, CUT)
            if n == 1 and i == 1:
                fetch(n, 3, b, block_at(2), dev(dx=3), CUT, SL - CUT)
            start(remote(mine, mine, *sems, dev(dc=1)))

        rows = lax.broadcasted_iota(jnp.int32, (NB, NB), 0)
        cols = lax.broadcasted_iota(jnp.int32, (NB, NB), 1)
        place = ((cols // 2) % 3) * 128 + ((cols // 6) % 2) * 64 + ((cols // 12) % 4) * 16 + (cols % 2) * 8 + cols // 48
        onehot[...] = jnp.where(rows == place, 1.0, 0.0).astype(BF16)

        for i in range(3):
            pl.semaphore_wait(relay.at[i], 1)
        tell(3, dz=2)
        tell(4, dz=6)
        for load in loads:
            load.wait()
        for i in (3, 4):
            pl.semaphore_wait(relay.at[i], 1)
        for t in range(3):
            for p in range(NP):

                def prepare(q, _, t=t, p=p):
                    for cc in range(2):
                        for yy in range(4):
                            row = yy * 12 + cc * 6 + 2 * t
                            v = jnp.concatenate([i32[p, q, pl.ds(row + r, 8, stride=48), :] for r in range(2)], axis=0)
                            hi, lo = split(v)
                            to = pl.ds(p * T + cc * 64 + yy * 16, 16)
                            lanes = pl.ds(pl.multiple_of(q * T, T), T)
                            ihi[t, to, lanes] = hi
                            ilo[t, to, lanes] = lo
                    return 0

                lax.fori_loop(0, 12, prepare, 0)

        def orbitals(n):
            for i in range(3 + n):
                forward(n, i)
            for i in range(3 + n):
                arrive(gather[n, i])
            for b in range(4):
                v = jnp.concatenate([cf[b, pl.ds(q * SL, SL), :] for q in (n, n + 2)], axis=0)
                hi, lo = split(v)
                chi[pl.ds(n * 2 * SL, 2 * SL), pl.ds(b * NB, NB)] = hi
                clo[pl.ds(n * 2 * SL, 2 * SL), pl.ds(b * NB, NB)] = lo

        def half(t, r0, nr):
            r = pl.ds(r0, nr)
            h[t, r, :] = nt(chi[r, :], ihi[t]) + nt(chi[r, :], ilo[t]) + nt(clo[r, :], ihi[t])

        odd = x % 2

        def row_of(j):
            q = (x + 2 + j) % 4
            return at(((q % 2) * 2 + q // 2) * SL)

        right, left = dev(dx=1), dev(dx=3)
        extra = row_of(jnp.where(c == 1, 3, 2)), dev(dx=jnp.where(c == 1, 1, 3))
        trade = {}

        def send(t, *ks):
            for k in ks:
                if k == "right0":
                    j, k, to = 2 - odd, 1 - odd, right
                elif k == "left0":
                    j, k, to = 3 * odd, 3 - odd, left
                elif k == "right1":
                    j, k, to = 1 + odd, odd, right
                elif k == "left1":
                    j, k, to = 3 - 3 * odd, 2 + odd, left
                else:
                    j, to = ((1, right), (2, right), (3, left), (0, left), (None, extra[1]))[k]
                row = extra[0] if j is None else row_of(j)
                copy = remote(h.at[t, pl.ds(row, SL)], xr.at[k, t], hsend.at[k, t], hrecv.at[k, t], to)
                copy.start()
                started.append(copy)
                trade.setdefault((t, ks[0]), []).append(copy)

        def sent(*which):
            for copy in trade.pop(which, []):
                copy.wait_send()
                started[:] = [p for p in started if p is not copy]

        def traded(t, k):
            return remote(h.at[t, pl.ds(0, SL)], xr.at[k, t], hsend.at[k, t], hrecv.at[k, t], right)

        orbitals(0)
        half(0, 0, 2 * SL)
        send(0, "right0", "left0")
        orbitals(1)
        half(0, 2 * SL, 2 * SL)
        send(0, "right1", "left1")
        send(0, 4)
        half(1, 0, 4 * SL)
        half(2, 0, 4 * SL)
        sent(0, "right0")

        pad = jnp.zeros((SLP - SL, T), F32)

        def operand(v, k, t, hi_ref, lo_ref):
            for p in range(NP):
                hi, lo = split(jnp.concatenate([v[:, p * T : (p + 1) * T], pad], axis=0))
                hi_ref[pl.ds(k * K + p * SLP, SLP), pl.ds(t * T, T)] = hi
                lo_ref[pl.ds(k * K + p * SLP, SLP), pl.ds(t * T, T)] = lo

        for t in range(3):
            for j in range(4):
                operand(h[t, pl.ds(row_of(j), SL), :], j, t, ohi, olo)

        def own(j, n):
            r = pl.ds(j * K, n * K)
            return ohi[r, :], olo[r, :]

        def got(k, n, t0, nt_):
            r, lanes = pl.ds(k * K, n * K), pl.ds(t0 * T, nt_ * T)
            return xhi[r, lanes], xlo[r, lanes]

        def put(rb, cb, r, cl, v):
            g[SLOT[rb, cb, r, cl]] = v

        pairs, ys, zsum = {}, {}, {}

        def pair_start(s):
            span = pl.ds(*SPANS[s])
            pairs[s] = remote(g.at[span, pl.ds(at((1 - c) * 64), 64)], gr.at[span], gsend.at[s], grecv.at[s], dev(dc=1))
            start(pairs[s])

        def pair_finish(s):
            arrive(pairs[s])
            span = pl.ds(*SPANS[s])
            keep = pl.ds(at(c * 64), 64)
            g[span, keep, :] += gr[span]
            for d in (1, 3, 2):
                there = pl.ds(at(c * 64 + ((y + d) % 4) * 16), 16)
                ys[s, d] = remote(g.at[span, there], yr.at[d - 1, span], ysend.at[d - 1, s], yrecv.at[d - 1, s], dev(dy=d))
                start(ys[s, d])

        def y_finish(s):
            for d in (1, 3, 2):
                arrive(ys[s, d])
            first, n = SPANS[s]
            span = pl.ds(first, n)
            v = g[span, pl.ds(at(c * 64 + y * 16), 16), :] + yr[0, span] + yr[1, span] + yr[2, span]
            ybuf[pl.ds(first * 16, n * 16), :] = v.reshape(n * 16, T)
            if s not in GSPANS:
                return
            g0, ng = GSPANS[s]
            for group in range(g0, g0 + ng):
                for zz in range(8):
                    zs[zz, group] = ybuf[pl.ds(group * 64 + zz, 8, stride=8), :]
            for d in (4, 3, 5, 2, 6, 1, 7):
                zsum[s, d] = remote(
                    zs.at[(z + d) % 8, pl.ds(g0, ng)], zr.at[d - 1, pl.ds(g0, ng)],
                    zsend.at[d - 1, s], zrecv.at[d - 1, s], dev(dz=d),
                )
                start(zsum[s, d])

        def z_finish(s):
            for d in range(1, 8):
                arrive(zsum[s, d])
            span = pl.ds(*GSPANS[s])
            v = zs[z, span]
            for d in range(7):
                v = v + zr[d, span]
            f[pl.ds(GSPANS[s][0] * 8, GSPANS[s][1] * 8), :] = v.reshape(GSPANS[s][1] * 8, T)

        ybuf[pl.ds(63 * 16, 16), :] = jnp.zeros((16, T), F32)
        sent(0, "right1")
        send(1, 1, 2)
        send(1, 4)
        v = gram(own(0, 4), own(0, 4))
        for r in range(3):
            for q in range(3):
                put(0, 0, r, q, v[r * T : (r + 1) * T, q * T : (q + 1) * T])
        pair_start(0)
        pair_finish(0)

        extra_k = pl.ds(pl.multiple_of(jnp.where(c == 1, 2 * K, 3 * K), 16), K)

        def take(t, ks):
            for k in ks:
                traded(t, k).wait_recv()
                operand(xr[k, t], k, t, xhi, xlo)

        def cross(d, t, v):
            for q in range(3):
                w = v[:, q * T : (q + 1) * T]
                put(d, 0, t, q, w)
                put(0, d, q, t, w.T)

        def far(d, t, v):
            for q in range(v.shape[1] // T):
                w = v[:, q * T : (q + 1) * T]
                put(d, -d, t, q, w)
                put(-d, d, q, t, w.T)

        def left_part(t):
            take(t, (1, 4))
            ve = gram(got(4, 1, t, 1), (ohi[extra_k, :], olo[extra_k, :]))
            v2 = gram(got(1, 1, t, 1), own(1, 1))
            cross(-1, t, v2 + jnp.where(c == 1, ve, 0.0))
            return jnp.where(c == 0, ve, 0.0)

        def right_part(t, ve):
            take(t, (2, 3))
            cross(1, t, gram(got(2, 2, t, 1), own(0, 2)) + ve)

        def far_part(t):
            take(t, (0,))
            far(-1, t, gram(got(0, 2, t, 1), got(2, 2, 0, t + 1)))
            if t > 0:
                far(1, t, gram(got(2, 2, t, 1), got(0, 2, 0, t)))

        sent(0, 4)
        send(1, 0, 3)
        for t in range(2):
            ve = left_part(t)
            right_part(t, ve)
            far_part(t)
            pair_start(t + 1)
            if t == 0:
                sent(1, 1)
                sent(1, 4)
                send(2, 1, 2)
                send(2, 4)
            y_finish(t)
            pair_finish(t + 1)
            if t == 0:
                sent(1, 0)
                send(2, 0, 3)
        ve = left_part(2)
        pair_start(3)
        right_part(2, ve)
        pair_finish(3)
        far_part(2)
        pair_start(4)
        y_finish(2)
        pair_finish(4)
        z_finish(0)
        z_finish(1)
        y_finish(3)
        z_finish(2)
        y_finish(4)
        z_finish(4)

        def strip(rb, cb, r):
            return jnp.concatenate([f[pl.ds(SLOT[rb, cb, r, q] * 2, 2), :] for q in range(3)], axis=1)

        def block(rb, cb):
            return jnp.concatenate([strip(rb, cb, r) for r in range(3)] + [jnp.zeros((2, NB), F32)], axis=0)

        def ordered(v):
            hi = v.astype(BF16)
            rest = v - hi.astype(F32)
            mid = rest.astype(BF16)
            low = (rest - mid.astype(F32)).astype(BF16)
            w = jnp.concatenate([hi.astype(F32), mid.astype(F32), low.astype(F32)], axis=0).astype(BF16)
            w = jnp.dot(w, onehot[...], preferred_element_type=F32)
            n = v.shape[0]
            return w[:n] + w[n : 2 * n] + w[2 * n :]

        for k, (rb, cb) in enumerate(((1, 0), (1, -1), (-1, 0), (-1, 1))):
            fs[k] = block(rb, cb)
        x_copies = [
            remote(fs.at[pl.ds(2 * k, 2)], fr.at[pl.ds(2 * k, 2)], xsend.at[k], xrecv.at[k], dev(dx=d))
            for k, d in ((0, 1), (1, 3))
        ]
        for copy in x_copies:
            start(copy)

        def lanes(d):
            return pl.ds(pl.multiple_of(((x + d) % 4) * NB, 128), NB)

        o_ref[:, lanes(0)] = ordered(block(0, 0))[:6]
        right_, left_ = block(0, 1), block(0, -1)
        for copy in x_copies:
            arrive(copy)
        v = ordered(jnp.concatenate([right_ + fr[2], fr[1] + fr[3], left_ + fr[0]], axis=0))
        for d in range(3):
            o_ref[:, lanes(d + 1)] = v[8 * d : 8 * d + 6]

    work()
    for copy in started:
        copy.wait_send()


def per_device(integrals, orbitals):
    dma = pltpu.SemaphoreType.DMA
    return pl.pallas_call(
        kernel,
        out_shape=jax.ShapeDtypeStruct((6, NL), F32),
        in_specs=[pl.BlockSpec(memory_space=pltpu.VMEM), pl.BlockSpec(memory_space=pl.ANY)],
        out_specs=pl.BlockSpec(memory_space=pltpu.VMEM),
        scratch_shapes=[
            pltpu.VMEM((NP, 12, NB, T), F32),
            pltpu.VMEM((3, NB, NL), BF16),
            pltpu.VMEM((3, NB, NL), BF16),
            pltpu.VMEM((4, 4 * SL, NB), F32),
            pltpu.VMEM((4 * SL, NL), BF16),
            pltpu.VMEM((4 * SL, NL), BF16),
            pltpu.VMEM((3, 4 * SL, NB), F32),
            pltpu.VMEM((5, 3, SL, NB), F32),
            pltpu.VMEM((4 * K, NB), BF16),
            pltpu.VMEM((4 * K, NB), BF16),
            pltpu.VMEM((5 * K, NB), BF16),
            pltpu.VMEM((5 * K, NB), BF16),
            pltpu.VMEM((63, T, T), F32),
            pltpu.VMEM((63, T // 2, T), F32),
            pltpu.VMEM((3, 63, 16, T), F32),
            pltpu.VMEM((1024, T), F32),
            pltpu.VMEM((8, 16, 8, T), F32),
            pltpu.VMEM((7, 16, 8, T), F32),
            pltpu.VMEM((128, T), F32),
            pltpu.VMEM((4, 8, NB), F32),
            pltpu.VMEM((4, 8, NB), F32),
            pltpu.VMEM((NB, NB), BF16),
            pltpu.SemaphoreType.REGULAR((5,)),
            dma((NP, 12)),
            dma((2, 4)), dma((2, 4)), dma((2, 4)), dma((2, 4)),
            dma((5, 3)), dma((5, 3)),
            dma((5,)), dma((5,)),
            dma((3, 5)), dma((3, 5)),
            dma((7, 5)), dma((7, 5)),
            dma((2,)), dma((2,)),
        ],
        compiler_params=pltpu.CompilerParams(
            collective_id=0, has_side_effects=True, vmem_limit_bytes=56 << 20
        ),
    )(orbitals.T, integrals)


def solution(mesh):
    return jax.shard_map(
        per_device,
        mesh=mesh,
        in_specs=(P("aux", "blk", None), P("blk", None)),
        out_specs=P(("blk", "aux"), None),
        check_vma=False,
    )
```

```python
import jax
import jax.numpy as jnp
from jax import lax
from jax.experimental import pallas as pl
from jax.experimental.pallas import tpu as pltpu
from jax.sharding import PartitionSpec as P

MESH = pl.DeviceIdType.MESH
F32 = jnp.float32
BF16 = jnp.bfloat16
NP = 3
NB = 384
NL = 1536
OCC = 400
SL = 104
SLP = 112
K = NP * SLP
T = 128


def tile_sets():
    sets = [[(0, 0, r, c) for r in range(3) for c in range(3)]]
    for t in range(3):
        left = [(0, -1, r, t) for r in range(3)] + [(-1, 0, t, c) for c in range(3)]
        rest = [(0, 1, r, t) for r in range(3)] + [(1, 0, t, c) for c in range(3)]
        for d in (-1, 1):
            rest += [(d, -d, t, c) for c in range(t + 1)] + [(d, -d, r, t) for r in range(t)]
        sets += [left, rest] if t == 2 else [left + rest]
    return sets


SETS = tile_sets()
SLOT = {tile: i for i, tile in enumerate(sum(SETS, []))}
ENDS = [sum(len(s) for s in SETS[: i + 1]) for i in range(len(SETS))]
SPANS = [(e - len(s), len(s)) for s, e in zip(SETS, ENDS)]
GSPANS = {0: (0, 2), 1: (2, 3), 2: (5, 5), 4: (10, 6)}


def split(v):
    hi = v.astype(BF16)
    return hi, (v - hi.astype(F32)).astype(BF16)


def nt(a, b):
    return lax.dot_general(a, b, (((1,), (1,)), ((), ())), preferred_element_type=F32)


def tn(a, b):
    return lax.dot_general(a, b, (((0,), (0,)), ((), ())), preferred_element_type=F32)


def gram(a, b):
    return tn(a[0], b[0]) + tn(a[0], b[1]) + tn(a[1], b[0])


def kernel(
    ct_ref, i_ref, o_ref,
    i32, ihi, ilo, cf, chi, clo, h, xr, ohi, olo, xhi, xlo,
    g, gr, yr, ybuf, zs, zr, f, fs, fr, onehot,
    relay, isem, csend, crecv, fsend, frecv, hsend, hrecv, gsend, grecv, ysend, yrecv, zsend, zrecv, xsend, xrecv,
):
    x = lax.axis_index("blk")
    a = lax.axis_index("aux")
    z, y, c = a // 8, (a // 2) % 4, a % 2
    started = []

    def dev(dx=0, dz=0, dy=0, dc=0):
        return ((x + dx) % 4, (((z + dz) % 8) * 4 + (y + dy) % 4) * 2 + (c + dc) % 2)

    def remote(src, dst, send, recv, to):
        return pltpu.make_async_remote_copy(
            src_ref=src, dst_ref=dst, send_sem=send, recv_sem=recv, device_id=to, device_id_type=MESH
        )

    def start(copy):
        copy.start()
        started.append(copy)

    def arrive(copy):
        copy.wait_recv()

    def at(row):
        return pl.multiple_of(row, 8)

    def work():
        loads = [
            pltpu.make_async_copy(i_ref.at[p, :, pl.ds(q * T, T)], i32.at[p, q], isem.at[p, q])
            for p in range(NP) for q in range(12)
        ]
        for load in loads:
            load.start()

        partners = [dict(dx=2), dict(dx=1), dict(dx=3), dict(dz=1), dict(dz=7), dict(dy=1), dict(dy=3), dict(dc=1)]
        barrier = pltpu.get_barrier_semaphore()
        for partner in partners:
            pl.semaphore_signal(barrier, inc=1, device_id=dev(**partner), device_id_type=MESH)
        cf[x, pl.ds(0, OCC), :] = ct_ref[...]
        cf[x, pl.ds(OCC, 4 * SL - OCC), :] = jnp.zeros((4 * SL - OCC, NB), F32)
        pl.semaphore_wait(barrier, len(partners))

        gather = {}

        def area(b, n, core, r0=0, nr=SL):
            return cf.at[b, pl.ds(at((2 * core + n) * SL + r0), nr)]

        def fetch(n, i, b, come, to, r0=0, nr=SL):
            mine, here = area(b, n, c, r0, nr), area(come, n, c, r0, nr)
            sems = csend.at[n, i], crecv.at[n, i]
            gather[n, i] = come, r0, nr, remote(here, here, *sems, to)
            start(remote(mine, mine, *sems, to))

        def block_at(dx):
            return (x + dx) % 4

        for n in range(2):
            fetch(n, 0, x, block_at(3), dev(dx=1))
            fetch(n, 1, x, block_at(1), dev(dx=3))
            fetch(n, 2, x, block_at(2), dev(dx=2))

        def tell(i, **to):
            pl.semaphore_signal(relay.at[i], inc=1, device_id=dev(**to), device_id_type=MESH)

        tell(0, dy=1)
        tell(1, dz=1)
        tell(2, dz=7)

        def forward(n, i):
            b, r0, nr, copy = gather[n, i]
            arrive(copy)
            mine, there = area(b, n, c, r0, nr), area(b, n, 1 - c, r0, nr)
            sems = fsend.at[n, i], frecv.at[n, i]
            gather[n, i] = remote(there, there, *sems, dev(dc=1))
            start(remote(mine, mine, *sems, dev(dc=1)))

        rows = lax.broadcasted_iota(jnp.int32, (NB, NB), 0)
        cols = lax.broadcasted_iota(jnp.int32, (NB, NB), 1)
        place = ((cols // 2) % 3) * 128 + ((cols // 6) % 2) * 64 + ((cols // 12) % 4) * 16 + (cols % 2) * 8 + cols // 48
        onehot[...] = jnp.where(rows == place, 1.0, 0.0).astype(BF16)

        for i in range(3):
            pl.semaphore_wait(relay.at[i], 1)
        tell(3, dz=2)
        tell(4, dz=6)
        for load in loads:
            load.wait()
        for i in (3, 4):
            pl.semaphore_wait(relay.at[i], 1)
        for t in range(3):
            for p in range(NP):

                def prepare(q, _, t=t, p=p):
                    for cc in range(2):
                        for yy in range(4):
                            row = yy * 12 + cc * 6 + 2 * t
                            v = jnp.concatenate([i32[p, q, pl.ds(row + r, 8, stride=48), :] for r in range(2)], axis=0)
                            hi, lo = split(v)
                            to = pl.ds(p * T + cc * 64 + yy * 16, 16)
                            lanes = pl.ds(pl.multiple_of(q * T, T), T)
                            ihi[t, to, lanes] = hi
                            ilo[t, to, lanes] = lo
                    return 0

                lax.fori_loop(0, 12, prepare, 0)

        def orbitals(n):
            for i in range(3):
                forward(n, i)
            for i in range(3):
                arrive(gather[n, i])
            for b in range(4):
                v = jnp.concatenate([cf[b, pl.ds(q * SL, SL), :] for q in (n, n + 2)], axis=0)
                hi, lo = split(v)
                chi[pl.ds(n * 2 * SL, 2 * SL), pl.ds(b * NB, NB)] = hi
                clo[pl.ds(n * 2 * SL, 2 * SL), pl.ds(b * NB, NB)] = lo

        def half(t, r0, nr):
            r = pl.ds(r0, nr)
            h[t, r, :] = nt(chi[r, :], ihi[t]) + nt(chi[r, :], ilo[t]) + nt(clo[r, :], ihi[t])

        odd = x % 2

        def row_of(j):
            q = (x + 2 + j) % 4
            return at(((q % 2) * 2 + q // 2) * SL)

        right, left = dev(dx=1), dev(dx=3)
        extra = row_of(jnp.where(c == 1, 3, 2)), dev(dx=jnp.where(c == 1, 1, 3))
        trade = {}

        def send(t, *ks):
            for k in ks:
                if k == "right0":
                    j, k, to = 2 - odd, 1 - odd, right
                elif k == "left0":
                    j, k, to = 3 * odd, 3 - odd, left
                elif k == "right1":
                    j, k, to = 1 + odd, odd, right
                elif k == "left1":
                    j, k, to = 3 - 3 * odd, 2 + odd, left
                else:
                    j, to = ((1, right), (2, right), (3, left), (0, left), (None, extra[1]))[k]
                row = extra[0] if j is None else row_of(j)
                copy = remote(h.at[t, pl.ds(row, SL)], xr.at[k, t], hsend.at[k, t], hrecv.at[k, t], to)
                copy.start()
                started.append(copy)
                trade.setdefault((t, ks[0]), []).append(copy)

        def sent(*which):
            for copy in trade.pop(which, []):
                copy.wait_send()
                started[:] = [p for p in started if p is not copy]

        def traded(t, k):
            return remote(h.at[t, pl.ds(0, SL)], xr.at[k, t], hsend.at[k, t], hrecv.at[k, t], right)

        orbitals(0)
        for t in range(3):
            half(t, 0, 2 * SL)
            if t < 2:
                send(t, "right0", "left0")
        orbitals(1)
        half(0, 2 * SL, 2 * SL)
        send(0, "right1", "left1")
        send(0, 4)
        half(1, 2 * SL, 2 * SL)
        half(2, 2 * SL, 2 * SL)

        pad = jnp.zeros((SLP - SL, T), F32)

        def operand(v, k, t, hi_ref, lo_ref):
            for p in range(NP):
                hi, lo = split(jnp.concatenate([v[:, p * T : (p + 1) * T], pad], axis=0))
                hi_ref[pl.ds(k * K + p * SLP, SLP), pl.ds(t * T, T)] = hi
                lo_ref[pl.ds(k * K + p * SLP, SLP), pl.ds(t * T, T)] = lo

        for t in range(3):
            for j in range(4):
                operand(h[t, pl.ds(row_of(j), SL), :], j, t, ohi, olo)

        def own(j, n):
            r = pl.ds(j * K, n * K)
            return ohi[r, :], olo[r, :]

        def got(k, n, t0, nt_):
            r, lanes = pl.ds(k * K, n * K), pl.ds(t0 * T, nt_ * T)
            return xhi[r, lanes], xlo[r, lanes]

        def put(rb, cb, r, cl, v):
            g[SLOT[rb, cb, r, cl]] = v

        pairs, ys, zsum = {}, {}, {}

        def pair_start(s):
            span = pl.ds(*SPANS[s])
            pairs[s] = remote(g.at[span, pl.ds(at((1 - c) * 64), 64)], gr.at[span], gsend.at[s], grecv.at[s], dev(dc=1))
            start(pairs[s])

        def pair_finish(s):
            arrive(pairs[s])
            span = pl.ds(*SPANS[s])
            keep = pl.ds(at(c * 64), 64)
            g[span, keep, :] += gr[span]
            for d in (1, 3, 2):
                there = pl.ds(at(c * 64 + ((y + d) % 4) * 16), 16)
                ys[s, d] = remote(g.at[span, there], yr.at[d - 1, span], ysend.at[d - 1, s], yrecv.at[d - 1, s], dev(dy=d))
                start(ys[s, d])

        def y_finish(s):
            for d in (1, 3, 2):
                arrive(ys[s, d])
            first, n = SPANS[s]
            span = pl.ds(first, n)
            v = g[span, pl.ds(at(c * 64 + y * 16), 16), :] + yr[0, span] + yr[1, span] + yr[2, span]
            ybuf[pl.ds(first * 16, n * 16), :] = v.reshape(n * 16, T)
            if s not in GSPANS:
                return
            g0, ng = GSPANS[s]
            for group in range(g0, g0 + ng):
                for zz in range(8):
                    zs[zz, group] = ybuf[pl.ds(group * 64 + zz, 8, stride=8), :]
            for d in (4, 3, 5, 2, 6, 1, 7):
                zsum[s, d] = remote(
                    zs.at[(z + d) % 8, pl.ds(g0, ng)], zr.at[d - 1, pl.ds(g0, ng)],
                    zsend.at[d - 1, s], zrecv.at[d - 1, s], dev(dz=d),
                )
                start(zsum[s, d])

        def z_finish(s):
            for d in range(1, 8):
                arrive(zsum[s, d])
            span = pl.ds(*GSPANS[s])
            v = zs[z, span]
            for d in range(7):
                v = v + zr[d, span]
            f[pl.ds(GSPANS[s][0] * 8, GSPANS[s][1] * 8), :] = v.reshape(GSPANS[s][1] * 8, T)

        ybuf[pl.ds(63 * 16, 16), :] = jnp.zeros((16, T), F32)
        v = gram(own(0, 4), own(0, 4))
        for r in range(3):
            for q in range(3):
                put(0, 0, r, q, v[r * T : (r + 1) * T, q * T : (q + 1) * T])
        pair_start(0)
        pair_finish(0)

        extra_k = pl.ds(pl.multiple_of(jnp.where(c == 1, 2 * K, 3 * K), 16), K)

        def take(t, ks):
            for k in ks:
                traded(t, k).wait_recv()
                operand(xr[k, t], k, t, xhi, xlo)

        def cross(d, t, v):
            for q in range(3):
                w = v[:, q * T : (q + 1) * T]
                put(d, 0, t, q, w)
                put(0, d, q, t, w.T)

        def far(d, t, v):
            for q in range(v.shape[1] // T):
                w = v[:, q * T : (q + 1) * T]
                put(d, -d, t, q, w)
                put(-d, d, q, t, w.T)

        def left_part(t):
            take(t, (1, 4))
            ve = gram(got(4, 1, t, 1), (ohi[extra_k, :], olo[extra_k, :]))
            v2 = gram(got(1, 1, t, 1), own(1, 1))
            cross(-1, t, v2 + jnp.where(c == 1, ve, 0.0))
            return jnp.where(c == 0, ve, 0.0)

        def right_part(t, ve):
            take(t, (2, 3))
            cross(1, t, gram(got(2, 2, t, 1), own(0, 2)) + ve)

        def far_part(t):
            take(t, (0,))
            far(-1, t, gram(got(0, 2, t, 1), got(2, 2, 0, t + 1)))
            if t > 0:
                far(1, t, gram(got(2, 2, t, 1), got(0, 2, 0, t)))

        sent(0, "right1")
        send(1, "right1", "left1")
        send(1, 4)

        right_part(0, left_part(0))
        far_part(0)
        pair_start(1)
        sent(1, "right1")
        send(2, 1, 2)
        send(2, 4)
        pair_finish(1)
        y_finish(0)

        ve = left_part(1)
        sent(2, 1)
        send(2, 0, 3)
        right_part(1, ve)
        far_part(1)
        pair_start(2)
        z_finish(0)
        pair_finish(2)

        ve = left_part(2)
        pair_start(3)
        y_finish(1)
        pair_finish(3)
        right_part(2, ve)
        far_part(2)
        pair_start(4)
        z_finish(1)
        pair_finish(4)
        y_finish(2)
        y_finish(3)
        y_finish(4)
        z_finish(2)
        z_finish(4)

        def strip(rb, cb, r):
            return jnp.concatenate([f[pl.ds(SLOT[rb, cb, r, q] * 2, 2), :] for q in range(3)], axis=1)

        def block(rb, cb):
            return jnp.concatenate([strip(rb, cb, r) for r in range(3)] + [jnp.zeros((2, NB), F32)], axis=0)

        def ordered(v):
            hi = v.astype(BF16)
            rest = v - hi.astype(F32)
            mid = rest.astype(BF16)
            low = (rest - mid.astype(F32)).astype(BF16)
            w = jnp.concatenate([hi.astype(F32), mid.astype(F32), low.astype(F32)], axis=0).astype(BF16)
            w = jnp.dot(w, onehot[...], preferred_element_type=F32)
            n = v.shape[0]
            return w[:n] + w[n : 2 * n] + w[2 * n :]

        for k, (rb, cb) in enumerate(((1, 0), (1, -1), (-1, 0), (-1, 1))):
            fs[k] = block(rb, cb)
        x_copies = [
            remote(fs.at[pl.ds(2 * k, 2)], fr.at[pl.ds(2 * k, 2)], xsend.at[k], xrecv.at[k], dev(dx=d))
            for k, d in ((0, 1), (1, 3))
        ]
        for copy in x_copies:
            start(copy)

        def lanes(d):
            return pl.ds(pl.multiple_of(((x + d) % 4) * NB, 128), NB)

        o_ref[:, lanes(0)] = ordered(block(0, 0))[:6]
        right_, left_ = block(0, 1), block(0, -1)
        for copy in x_copies:
            arrive(copy)
        v = ordered(jnp.concatenate([right_ + fr[2], fr[1] + fr[3], left_ + fr[0]], axis=0))
        for d in range(3):
            o_ref[:, lanes(d + 1)] = v[8 * d : 8 * d + 6]

    work()
    for copy in started:
        copy.wait_send()


def per_device(integrals, orbitals):
    dma = pltpu.SemaphoreType.DMA
    return pl.pallas_call(
        kernel,
        out_shape=jax.ShapeDtypeStruct((6, NL), F32),
        in_specs=[pl.BlockSpec(memory_space=pltpu.VMEM), pl.BlockSpec(memory_space=pl.ANY)],
        out_specs=pl.BlockSpec(memory_space=pltpu.VMEM),
        scratch_shapes=[
            pltpu.VMEM((NP, 12, NB, T), F32),
            pltpu.VMEM((3, NB, NL), BF16),
            pltpu.VMEM((3, NB, NL), BF16),
            pltpu.VMEM((4, 4 * SL, NB), F32),
            pltpu.VMEM((4 * SL, NL), BF16),
            pltpu.VMEM((4 * SL, NL), BF16),
            pltpu.VMEM((3, 4 * SL, NB), F32),
            pltpu.VMEM((5, 3, SL, NB), F32),
            pltpu.VMEM((4 * K, NB), BF16),
            pltpu.VMEM((4 * K, NB), BF16),
            pltpu.VMEM((5 * K, NB), BF16),
            pltpu.VMEM((5 * K, NB), BF16),
            pltpu.VMEM((63, T, T), F32),
            pltpu.VMEM((63, T // 2, T), F32),
            pltpu.VMEM((3, 63, 16, T), F32),
            pltpu.VMEM((1024, T), F32),
            pltpu.VMEM((8, 16, 8, T), F32),
            pltpu.VMEM((7, 16, 8, T), F32),
            pltpu.VMEM((128, T), F32),
            pltpu.VMEM((4, 8, NB), F32),
            pltpu.VMEM((4, 8, NB), F32),
            pltpu.VMEM((NB, NB), BF16),
            pltpu.SemaphoreType.REGULAR((5,)),
            dma((NP, 12)),
            dma((2, 3)), dma((2, 3)), dma((2, 3)), dma((2, 3)),
            dma((5, 3)), dma((5, 3)),
            dma((5,)), dma((5,)),
            dma((3, 5)), dma((3, 5)),
            dma((7, 5)), dma((7, 5)),
            dma((2,)), dma((2,)),
        ],
        compiler_params=pltpu.CompilerParams(
            collective_id=0, has_side_effects=True, vmem_limit_bytes=56 << 20
        ),
    )(orbitals.T, integrals)


def solution(mesh):
    return jax.shard_map(
        per_device,
        mesh=mesh,
        in_specs=(P("aux", "blk", None), P("blk", None)),
        out_specs=P(("blk", "aux"), None),
        check_vma=False,
    )
```

```python
import jax
import jax.numpy as jnp
from jax import lax
from jax.experimental import pallas as pl
from jax.experimental.pallas import tpu as pltpu
from jax.sharding import PartitionSpec as P

MESH = pl.DeviceIdType.MESH
F32 = jnp.float32
BF16 = jnp.bfloat16
NP = 3
NB = 384
NL = 1536
OCC = 400
SL = 104
SLP = 112
K = NP * SLP
T = 128


def tile_sets():
    sets = [[(0, 0, r, c) for r in range(3) for c in range(3)]]
    for t in range(3):
        left = [(0, -1, r, t) for r in range(3)] + [(-1, 0, t, c) for c in range(3)]
        rest = [(0, 1, r, t) for r in range(3)] + [(1, 0, t, c) for c in range(3)]
        for d in (-1, 1):
            rest += [(d, -d, t, c) for c in range(t + 1)] + [(d, -d, r, t) for r in range(t)]
        sets += [left, rest] if t == 2 else [left + rest]
    return sets


SETS = tile_sets()
SLOT = {tile: i for i, tile in enumerate(sum(SETS, []))}
ENDS = [sum(len(s) for s in SETS[: i + 1]) for i in range(len(SETS))]
SPANS = [(e - len(s), len(s)) for s, e in zip(SETS, ENDS)]
GSPANS = {0: (0, 2), 1: (2, 3), 2: (5, 5), 4: (10, 6)}


def split(v):
    hi = v.astype(BF16)
    return hi, (v - hi.astype(F32)).astype(BF16)


def nt(a, b):
    return lax.dot_general(a, b, (((1,), (1,)), ((), ())), preferred_element_type=F32)


def tn(a, b):
    return lax.dot_general(a, b, (((0,), (0,)), ((), ())), preferred_element_type=F32)


def gram(a, b):
    return tn(a[0], b[0]) + tn(a[0], b[1]) + tn(a[1], b[0])


def kernel(
    ct_ref, i_ref, o_ref,
    i32, ihi, ilo, cf, chi, clo, h, xr, ohi, olo, xhi, xlo,
    g, gr, yr, ybuf, zs, zr, f, fs, fr, onehot,
    relay, isem, csend, crecv, fsend, frecv, hsend, hrecv, gsend, grecv, ysend, yrecv, zsend, zrecv, xsend, xrecv,
):
    x = lax.axis_index("blk")
    a = lax.axis_index("aux")
    z, y, c = a // 8, (a // 2) % 4, a % 2
    started = []

    def dev(dx=0, dz=0, dy=0, dc=0):
        return ((x + dx) % 4, (((z + dz) % 8) * 4 + (y + dy) % 4) * 2 + (c + dc) % 2)

    def remote(src, dst, send, recv, to):
        return pltpu.make_async_remote_copy(
            src_ref=src, dst_ref=dst, send_sem=send, recv_sem=recv, device_id=to, device_id_type=MESH
        )

    def start(copy):
        copy.start()
        started.append(copy)

    def drain():
        for copy in started:
            copy.wait_send()
        started.clear()

    def arrive(copy):
        copy.wait_recv()

    def at(row):
        return pl.multiple_of(row, 8)

    def work():
        loads = [
            pltpu.make_async_copy(i_ref.at[p, :, pl.ds(q * T, T)], i32.at[p, q], isem.at[p, q])
            for p in range(NP) for q in range(12)
        ]
        for load in loads:
            load.start()

        partners = [dict(dx=2), dict(dx=1), dict(dx=3), dict(dz=1), dict(dz=7), dict(dy=1), dict(dy=3), dict(dc=1)]
        barrier = pltpu.get_barrier_semaphore()
        for partner in partners:
            pl.semaphore_signal(barrier, inc=1, device_id=dev(**partner), device_id_type=MESH)
        cf[x, pl.ds(0, OCC), :] = ct_ref[...]
        cf[x, pl.ds(OCC, 4 * SL - OCC), :] = jnp.zeros((4 * SL - OCC, NB), F32)
        pl.semaphore_wait(barrier, len(partners))

        gather = {}

        def area(b, n, core, r0=0, nr=SL):
            return cf.at[b, pl.ds(at((2 * core + n) * SL + r0), nr)]

        def fetch(n, i, b, come, to, r0=0, nr=SL):
            mine, here = area(b, n, c, r0, nr), area(come, n, c, r0, nr)
            sems = csend.at[n, i], crecv.at[n, i]
            gather[n, i] = come, r0, nr, remote(here, here, *sems, to)
            start(remote(mine, mine, *sems, to))

        def block_at(dx):
            return (x + dx) % 4

        def fetch_all(n):
            fetch(n, 2, x, block_at(2), dev(dx=2))
            fetch(n, 0, x, block_at(3), dev(dx=1))
            fetch(n, 1, x, block_at(1), dev(dx=3))

        fetch_all(0)

        def tell(i, **to):
            pl.semaphore_signal(relay.at[i], inc=1, device_id=dev(**to), device_id_type=MESH)

        tell(0, dy=1)
        tell(1, dz=1)
        tell(2, dz=7)

        def forward(n, i):
            b, r0, nr, copy = gather[n, i]
            arrive(copy)
            mine, there = area(b, n, c, r0, nr), area(b, n, 1 - c, r0, nr)
            sems = fsend.at[n, i], frecv.at[n, i]
            gather[n, i] = remote(there, there, *sems, dev(dc=1))
            start(remote(mine, mine, *sems, dev(dc=1)))

        rows = lax.broadcasted_iota(jnp.int32, (NB, NB), 0)
        cols = lax.broadcasted_iota(jnp.int32, (NB, NB), 1)
        place = ((cols // 2) % 3) * 128 + ((cols // 6) % 2) * 64 + ((cols // 12) % 4) * 16 + (cols % 2) * 8 + cols // 48
        onehot[...] = jnp.where(rows == place, 1.0, 0.0).astype(BF16)

        for i in range(3):
            pl.semaphore_wait(relay.at[i], 1)
        fetch_all(1)
        tell(3, dz=2)
        tell(4, dz=6)
        for load in loads:
            load.wait()
        for i in (3, 4):
            pl.semaphore_wait(relay.at[i], 1)
        for t in range(3):
            for p in range(NP):

                def prepare(q, _, t=t, p=p):
                    for cc in range(2):
                        for yy in range(4):
                            row = yy * 12 + cc * 6 + 2 * t
                            v = jnp.concatenate([i32[p, q, pl.ds(row + r, 8, stride=48), :] for r in range(2)], axis=0)
                            hi, lo = split(v)
                            to = pl.ds(p * T + cc * 64 + yy * 16, 16)
                            lanes = pl.ds(pl.multiple_of(q * T, T), T)
                            ihi[t, to, lanes] = hi
                            ilo[t, to, lanes] = lo
                    return 0

                lax.fori_loop(0, 12, prepare, 0)

        def orbitals(n):
            for i in range(3):
                forward(n, i)
            for i in range(3):
                arrive(gather[n, i])
            for b in range(4):
                v = jnp.concatenate([cf[b, pl.ds(q * SL, SL), :] for q in (n, n + 2)], axis=0)
                hi, lo = split(v)
                chi[pl.ds(n * 2 * SL, 2 * SL), pl.ds(b * NB, NB)] = hi
                clo[pl.ds(n * 2 * SL, 2 * SL), pl.ds(b * NB, NB)] = lo

        def half(t, r0, nr):
            r = pl.ds(r0, nr)
            h[t, r, :] = nt(chi[r, :], ihi[t]) + nt(chi[r, :], ilo[t]) + nt(clo[r, :], ihi[t])

        odd = x % 2

        def row_of(j):
            q = (x + 2 + j) % 4
            return at(((q % 2) * 2 + q // 2) * SL)

        right, left = dev(dx=1), dev(dx=3)
        extra = row_of(jnp.where(c == 1, 3, 2)), dev(dx=jnp.where(c == 1, 1, 3))
        trade = {}

        def send(t, *ks):
            for k in ks:
                if k == "right0":
                    j, k, to = 2 - odd, 1 - odd, right
                elif k == "left0":
                    j, k, to = 3 * odd, 3 - odd, left
                elif k == "right1":
                    j, k, to = 1 + odd, odd, right
                elif k == "left1":
                    j, k, to = 3 - 3 * odd, 2 + odd, left
                else:
                    j, to = ((1, right), (2, right), (3, left), (0, left), (None, extra[1]))[k]
                row = extra[0] if j is None else row_of(j)
                copy = remote(h.at[t, pl.ds(row, SL)], xr.at[k, t], hsend.at[k, t], hrecv.at[k, t], to)
                copy.start()
                started.append(copy)
                trade.setdefault((t, ks[0]), []).append(copy)

        def sent(*which):
            for copy in trade.pop(which, []):
                copy.wait_send()
                started[:] = [p for p in started if p is not copy]

        def traded(t, k):
            return remote(h.at[t, pl.ds(0, SL)], xr.at[k, t], hsend.at[k, t], hrecv.at[k, t], right)

        orbitals(0)
        for t in range(3):
            half(t, 0, 2 * SL)
            if t < 2:
                send(t, "right0", "left0")
        orbitals(1)
        half(0, 2 * SL, 2 * SL)
        send(0, "right1", "left1")
        send(0, 4)
        half(1, 2 * SL, 2 * SL)
        half(2, 2 * SL, 2 * SL)

        pad = jnp.zeros((SLP - SL, T), F32)

        def operand(v, k, t, hi_ref, lo_ref):
            for p in range(NP):
                hi, lo = split(jnp.concatenate([v[:, p * T : (p + 1) * T], pad], axis=0))
                hi_ref[pl.ds(k * K + p * SLP, SLP), pl.ds(t * T, T)] = hi
                lo_ref[pl.ds(k * K + p * SLP, SLP), pl.ds(t * T, T)] = lo

        for t in range(3):
            for j in range(4):
                operand(h[t, pl.ds(row_of(j), SL), :], j, t, ohi, olo)

        def own(j, n):
            r = pl.ds(j * K, n * K)
            return ohi[r, :], olo[r, :]

        def got(k, n, t0, nt_):
            r, lanes = pl.ds(k * K, n * K), pl.ds(t0 * T, nt_ * T)
            return xhi[r, lanes], xlo[r, lanes]

        def put(rb, cb, r, cl, v):
            g[SLOT[rb, cb, r, cl]] = v

        pairs, ys, zsum = {}, {}, {}

        def pair_start(s):
            span = pl.ds(*SPANS[s])
            pairs[s] = remote(g.at[span, pl.ds(at((1 - c) * 64), 64)], gr.at[span], gsend.at[s], grecv.at[s], dev(dc=1))
            start(pairs[s])

        def pair_finish(s):
            arrive(pairs[s])
            span = pl.ds(*SPANS[s])
            keep = pl.ds(at(c * 64), 64)
            g[span, keep, :] += gr[span]
            for d in (2, 1, 3):
                there = pl.ds(at(c * 64 + ((y + d) % 4) * 16), 16)
                ys[s, d] = remote(g.at[span, there], yr.at[d - 1, span], ysend.at[d - 1, s], yrecv.at[d - 1, s], dev(dy=d))
                start(ys[s, d])

        def y_finish(s):
            for d in (1, 3, 2):
                arrive(ys[s, d])
            first, n = SPANS[s]
            span = pl.ds(first, n)
            v = g[span, pl.ds(at(c * 64 + y * 16), 16), :] + yr[0, span] + yr[1, span] + yr[2, span]
            ybuf[pl.ds(first * 16, n * 16), :] = v.reshape(n * 16, T)
            if s not in GSPANS:
                return
            g0, ng = GSPANS[s]
            for group in range(g0, g0 + ng):
                for zz in range(8):
                    zs[zz, group] = ybuf[pl.ds(group * 64 + zz, 8, stride=8), :]
            for d in (4, 3, 5, 2, 6, 1, 7):
                zsum[s, d] = remote(
                    zs.at[(z + d) % 8, pl.ds(g0, ng)], zr.at[d - 1, pl.ds(g0, ng)],
                    zsend.at[d - 1, s], zrecv.at[d - 1, s], dev(dz=d),
                )
                start(zsum[s, d])

        def z_finish(s):
            for d in range(1, 8):
                arrive(zsum[s, d])
            span = pl.ds(*GSPANS[s])
            v = zs[z, span]
            for d in range(7):
                v = v + zr[d, span]
            f[pl.ds(GSPANS[s][0] * 8, GSPANS[s][1] * 8), :] = v.reshape(GSPANS[s][1] * 8, T)

        ybuf[pl.ds(63 * 16, 16), :] = jnp.zeros((16, T), F32)
        v = gram(own(0, 4), own(0, 4))
        for r in range(3):
            for q in range(3):
                put(0, 0, r, q, v[r * T : (r + 1) * T, q * T : (q + 1) * T])
        pair_start(0)
        pair_finish(0)

        extra_k = pl.ds(pl.multiple_of(jnp.where(c == 1, 2 * K, 3 * K), 16), K)

        def take(t, ks):
            for k in ks:
                traded(t, k).wait_recv()
                operand(xr[k, t], k, t, xhi, xlo)

        def cross(d, t, v):
            for q in range(3):
                w = v[:, q * T : (q + 1) * T]
                put(d, 0, t, q, w)
                put(0, d, q, t, w.T)

        def far(d, t, v):
            for q in range(v.shape[1] // T):
                w = v[:, q * T : (q + 1) * T]
                put(d, -d, t, q, w)
                put(-d, d, q, t, w.T)

        def left_part(t):
            take(t, (1, 4))
            ve = gram(got(4, 1, t, 1), (ohi[extra_k, :], olo[extra_k, :]))
            v2 = gram(got(1, 1, t, 1), own(1, 1))
            cross(-1, t, v2 + jnp.where(c == 1, ve, 0.0))
            return jnp.where(c == 0, ve, 0.0)

        def right_part(t, ve):
            take(t, (2, 3))
            cross(1, t, gram(got(2, 2, t, 1), own(0, 2)) + ve)

        def far_part(t):
            take(t, (0,))
            far(-1, t, gram(got(0, 2, t, 1), got(2, 2, 0, t + 1)))
            if t > 0:
                far(1, t, gram(got(2, 2, t, 1), got(0, 2, 0, t)))

        sent(0, "right1")
        send(1, "right1", "left1")
        send(1, 4)

        right_part(0, left_part(0))
        far_part(0)
        pair_start(1)
        sent(1, "right1")
        send(2, 1, 2)
        send(2, 4)
        pair_finish(1)
        y_finish(0)

        ve = left_part(1)
        send(2, 0, 3)
        right_part(1, ve)
        far_part(1)
        pair_start(2)
        z_finish(0)
        pair_finish(2)

        ve = left_part(2)
        pair_start(3)
        y_finish(1)
        pair_finish(3)
        right_part(2, ve)
        far_part(2)
        pair_start(4)
        z_finish(1)
        pair_finish(4)
        y_finish(2)
        y_finish(3)
        drain()
        y_finish(4)
        z_finish(2)
        z_finish(4)

        def strip(rb, cb, r):
            return jnp.concatenate([f[pl.ds(SLOT[rb, cb, r, q] * 2, 2), :] for q in range(3)], axis=1)

        def block(rb, cb):
            return jnp.concatenate([strip(rb, cb, r) for r in range(3)] + [jnp.zeros((2, NB), F32)], axis=0)

        def ordered(v):
            hi = v.astype(BF16)
            rest = v - hi.astype(F32)
            mid = rest.astype(BF16)
            low = (rest - mid.astype(F32)).astype(BF16)
            w = jnp.concatenate([hi.astype(F32), mid.astype(F32), low.astype(F32)], axis=0).astype(BF16)
            w = jnp.dot(w, onehot[...], preferred_element_type=F32)
            n = v.shape[0]
            return w[:n] + w[n : 2 * n] + w[2 * n :]

        for k, (rb, cb) in enumerate(((1, 0), (1, -1), (-1, 0), (-1, 1))):
            fs[k] = block(rb, cb)
        x_copies = [
            remote(fs.at[pl.ds(2 * k, 2)], fr.at[pl.ds(2 * k, 2)], xsend.at[k], xrecv.at[k], dev(dx=d))
            for k, d in ((0, 1), (1, 3))
        ]
        for copy in x_copies:
            start(copy)

        def lanes(d):
            return pl.ds(pl.multiple_of(((x + d) % 4) * NB, 128), NB)

        last = started[-2:]
        del started[-2:]
        drain()
        started.extend(last)
        o_ref[:, lanes(0)] = ordered(block(0, 0))[:6]
        right_, left_ = block(0, 1), block(0, -1)
        for copy in x_copies:
            arrive(copy)
        v = ordered(jnp.concatenate([right_ + fr[2], fr[1] + fr[3], left_ + fr[0]], axis=0))
        for d in range(3):
            o_ref[:, lanes(d + 1)] = v[8 * d : 8 * d + 6]

    work()
    drain()


def per_device(integrals, orbitals):
    dma = pltpu.SemaphoreType.DMA
    return pl.pallas_call(
        kernel,
        out_shape=jax.ShapeDtypeStruct((6, NL), F32),
        in_specs=[pl.BlockSpec(memory_space=pltpu.VMEM), pl.BlockSpec(memory_space=pl.ANY)],
        out_specs=pl.BlockSpec(memory_space=pltpu.VMEM),
        scratch_shapes=[
            pltpu.VMEM((NP, 12, NB, T), F32),
            pltpu.VMEM((3, NB, NL), BF16),
            pltpu.VMEM((3, NB, NL), BF16),
            pltpu.VMEM((4, 4 * SL, NB), F32),
            pltpu.VMEM((4 * SL, NL), BF16),
            pltpu.VMEM((4 * SL, NL), BF16),
            pltpu.VMEM((3, 4 * SL, NB), F32),
            pltpu.VMEM((5, 3, SL, NB), F32),
            pltpu.VMEM((4 * K, NB), BF16),
            pltpu.VMEM((4 * K, NB), BF16),
            pltpu.VMEM((5 * K, NB), BF16),
            pltpu.VMEM((5 * K, NB), BF16),
            pltpu.VMEM((63, T, T), F32),
            pltpu.VMEM((63, T // 2, T), F32),
            pltpu.VMEM((3, 63, 16, T), F32),
            pltpu.VMEM((1024, T), F32),
            pltpu.VMEM((8, 16, 8, T), F32),
            pltpu.VMEM((7, 16, 8, T), F32),
            pltpu.VMEM((128, T), F32),
            pltpu.VMEM((4, 8, NB), F32),
            pltpu.VMEM((4, 8, NB), F32),
            pltpu.VMEM((NB, NB), BF16),
            pltpu.SemaphoreType.REGULAR((5,)),
            dma((NP, 12)),
            dma((2, 3)), dma((2, 3)), dma((2, 3)), dma((2, 3)),
            dma((5, 3)), dma((5, 3)),
            dma((5,)), dma((5,)),
            dma((3, 5)), dma((3, 5)),
            dma((7, 5)), dma((7, 5)),
            dma((2,)), dma((2,)),
        ],
        compiler_params=pltpu.CompilerParams(
            collective_id=0, has_side_effects=True, vmem_limit_bytes=56 << 20
        ),
    )(orbitals.T, integrals)


def solution(mesh):
    return jax.shard_map(
        per_device,
        mesh=mesh,
        in_specs=(P("aux", "blk", None), P("blk", None)),
        out_specs=P(("blk", "aux"), None),
        check_vma=False,
    )
```

```python
import jax
import jax.numpy as jnp
from jax import lax
from jax.experimental import pallas as pl
from jax.experimental.pallas import tpu as pltpu
from jax.sharding import PartitionSpec as P

MESH = pl.DeviceIdType.MESH
F32 = jnp.float32
BF16 = jnp.bfloat16
NP = 3
NB = 384
NL = 1536
OCC = 400
SL = 104
SLP = 112
K = NP * SLP
T = 128


def tile_sets():
    sets = [[(0, 0, r, c) for r in range(3) for c in range(3)]]
    for t in range(3):
        left = [(0, -1, r, t) for r in range(3)] + [(-1, 0, t, c) for c in range(3)]
        rest = [(0, 1, r, t) for r in range(3)] + [(1, 0, t, c) for c in range(3)]
        for d in (-1, 1):
            rest += [(d, -d, t, c) for c in range(t + 1)] + [(d, -d, r, t) for r in range(t)]
        sets += [left, rest] if t == 2 else [left + rest]
    return sets


SETS = tile_sets()
SLOT = {tile: i for i, tile in enumerate(sum(SETS, []))}
ENDS = [sum(len(s) for s in SETS[: i + 1]) for i in range(len(SETS))]
SPANS = [(e - len(s), len(s)) for s, e in zip(SETS, ENDS)]
GSPANS = {0: (0, 2), 1: (2, 3), 2: (5, 5), 4: (10, 6)}


def split(v):
    hi = v.astype(BF16)
    return hi, (v - hi.astype(F32)).astype(BF16)


def nt(a, b):
    return lax.dot_general(a, b, (((1,), (1,)), ((), ())), preferred_element_type=F32)


def tn(a, b):
    return lax.dot_general(a, b, (((0,), (0,)), ((), ())), preferred_element_type=F32)


def gram(a, b):
    return tn(a[0], b[0]) + tn(a[0], b[1]) + tn(a[1], b[0])


def kernel(
    ct_ref, i_ref, o_ref,
    i32, ihi, ilo, cf, chi, clo, h, xr, ohi, olo, xhi, xlo,
    g, gr, yr, ybuf, zs, zr, f, fs, fr, onehot,
    relay, isem, csend, crecv, fsend, frecv, hsend, hrecv, gsend, grecv, ysend, yrecv, zsend, zrecv, xsend, xrecv,
):
    x = lax.axis_index("blk")
    a = lax.axis_index("aux")
    z, y, c = a // 8, (a // 2) % 4, a % 2
    started = []

    def dev(dx=0, dz=0, dy=0, dc=0):
        return ((x + dx) % 4, (((z + dz) % 8) * 4 + (y + dy) % 4) * 2 + (c + dc) % 2)

    def remote(src, dst, send, recv, to):
        return pltpu.make_async_remote_copy(
            src_ref=src, dst_ref=dst, send_sem=send, recv_sem=recv, device_id=to, device_id_type=MESH
        )

    def start(copy):
        copy.start()
        started.append(copy)

    def drain():
        for copy in started:
            copy.wait_send()
        started.clear()

    def arrive(copy):
        copy.wait_recv()

    def at(row):
        return pl.multiple_of(row, 8)

    def work():
        loads = [
            pltpu.make_async_copy(i_ref.at[p, :, pl.ds(q * T, T)], i32.at[p, q], isem.at[p, q])
            for p in range(NP) for q in range(12)
        ]
        for load in loads:
            load.start()

        partners = [dict(dx=2), dict(dx=1), dict(dx=3), dict(dz=1), dict(dz=7), dict(dy=1), dict(dy=3), dict(dc=1)]
        barrier = pltpu.get_barrier_semaphore()
        for partner in partners:
            pl.semaphore_signal(barrier, inc=1, device_id=dev(**partner), device_id_type=MESH)
        cf[x, pl.ds(0, OCC), :] = ct_ref[...]
        cf[x, pl.ds(OCC, 4 * SL - OCC), :] = jnp.zeros((4 * SL - OCC, NB), F32)
        pl.semaphore_wait(barrier, len(partners))

        gather = {}

        def area(b, n, core, r0=0, nr=SL):
            return cf.at[b, pl.ds(at((2 * core + n) * SL + r0), nr)]

        def fetch(n, i, b, come, to, r0=0, nr=SL):
            mine, here = area(b, n, c, r0, nr), area(come, n, c, r0, nr)
            sems = csend.at[n, i], crecv.at[n, i]
            gather[n, i] = come, r0, nr, remote(here, here, *sems, to)
            start(remote(mine, mine, *sems, to))

        def block_at(dx):
            return (x + dx) % 4

        def fetch_all(n):
            fetch(n, 2, x, block_at(2), dev(dx=2))
            fetch(n, 0, x, block_at(3), dev(dx=1))
            fetch(n, 1, x, block_at(1), dev(dx=3))

        fetch_all(0)

        def tell(i, **to):
            pl.semaphore_signal(relay.at[i], inc=1, device_id=dev(**to), device_id_type=MESH)

        tell(0, dy=1)
        tell(1, dz=1)
        tell(2, dz=7)

        def forward(n, i):
            b, r0, nr, copy = gather[n, i]
            arrive(copy)
            mine, there = area(b, n, c, r0, nr), area(b, n, 1 - c, r0, nr)
            sems = fsend.at[n, i], frecv.at[n, i]
            gather[n, i] = remote(there, there, *sems, dev(dc=1))
            start(remote(mine, mine, *sems, dev(dc=1)))

        rows = lax.broadcasted_iota(jnp.int32, (NB, NB), 0)
        cols = lax.broadcasted_iota(jnp.int32, (NB, NB), 1)
        place = ((cols // 2) % 3) * 128 + ((cols // 6) % 2) * 64 + ((cols // 12) % 4) * 16 + (cols % 2) * 8 + cols // 48
        onehot[...] = jnp.where(rows == place, 1.0, 0.0).astype(BF16)

        for i in range(3):
            pl.semaphore_wait(relay.at[i], 1)
        fetch_all(1)
        tell(3, dz=2)
        tell(4, dz=6)
        for load in loads:
            load.wait()
        for i in (3, 4):
            pl.semaphore_wait(relay.at[i], 1)
        for t in range(3):
            for p in range(NP):

                def prepare(q, _, t=t, p=p):
                    for cc in range(2):
                        for yy in range(4):
                            row = yy * 12 + cc * 6 + 2 * t
                            v = jnp.concatenate([i32[p, q, pl.ds(row + r, 8, stride=48), :] for r in range(2)], axis=0)
                            hi, lo = split(v)
                            to = pl.ds(p * T + cc * 64 + yy * 16, 16)
                            lanes = pl.ds(pl.multiple_of(q * T, T), T)
                            ihi[t, to, lanes] = hi
                            ilo[t, to, lanes] = lo
                    return 0

                lax.fori_loop(0, 12, prepare, 0)

        def orbitals(n):
            for i in range(3):
                forward(n, i)
            for i in range(3):
                arrive(gather[n, i])
            for b in range(4):
                v = jnp.concatenate([cf[b, pl.ds(q * SL, SL), :] for q in (n, n + 2)], axis=0)
                hi, lo = split(v)
                chi[pl.ds(n * 2 * SL, 2 * SL), pl.ds(b * NB, NB)] = hi
                clo[pl.ds(n * 2 * SL, 2 * SL), pl.ds(b * NB, NB)] = lo

        def half(t, r0, nr):
            r = pl.ds(r0, nr)
            h[t, r, :] = nt(chi[r, :], ihi[t]) + nt(chi[r, :], ilo[t]) + nt(clo[r, :], ihi[t])

        odd = x % 2

        def row_of(j):
            q = (x + 2 + j) % 4
            return at(((q % 2) * 2 + q // 2) * SL)

        right, left = dev(dx=1), dev(dx=3)
        extra = row_of(jnp.where(c == 1, 3, 2)), dev(dx=jnp.where(c == 1, 1, 3))
        trade = {}

        def send(t, *ks):
            for k in ks:
                if k == "right0":
                    j, k, to = 2 - odd, 1 - odd, right
                elif k == "left0":
                    j, k, to = 3 * odd, 3 - odd, left
                elif k == "right1":
                    j, k, to = 1 + odd, odd, right
                elif k == "left1":
                    j, k, to = 3 - 3 * odd, 2 + odd, left
                else:
                    j, to = ((1, right), (2, right), (3, left), (0, left), (None, extra[1]))[k]
                row = extra[0] if j is None else row_of(j)
                copy = remote(h.at[t, pl.ds(row, SL)], xr.at[k, t], hsend.at[k, t], hrecv.at[k, t], to)
                copy.start()
                started.append(copy)
                trade.setdefault((t, ks[0]), []).append(copy)

        def sent(*which):
            for copy in trade.pop(which, []):
                copy.wait_send()
                started[:] = [p for p in started if p is not copy]

        def traded(t, k):
            return remote(h.at[t, pl.ds(0, SL)], xr.at[k, t], hsend.at[k, t], hrecv.at[k, t], right)

        orbitals(0)
        for t in range(3):
            half(t, 0, 2 * SL)
            if t < 2:
                send(t, "right0", "left0")
        orbitals(1)
        half(0, 2 * SL, 2 * SL)
        send(0, "right1", "left1")
        send(0, 4)
        half(1, 2 * SL, 2 * SL)
        half(2, 2 * SL, 2 * SL)

        pad = jnp.zeros((SLP - SL, T), F32)

        def operand(v, k, t, hi_ref, lo_ref):
            for p in range(NP):
                hi, lo = split(jnp.concatenate([v[:, p * T : (p + 1) * T], pad], axis=0))
                hi_ref[pl.ds(k * K + p * SLP, SLP), pl.ds(t * T, T)] = hi
                lo_ref[pl.ds(k * K + p * SLP, SLP), pl.ds(t * T, T)] = lo

        for t in range(3):
            for j in range(4):
                operand(h[t, pl.ds(row_of(j), SL), :], j, t, ohi, olo)

        def own(j, n):
            r = pl.ds(j * K, n * K)
            return ohi[r, :], olo[r, :]

        def got(k, n, t0, nt_):
            r, lanes = pl.ds(k * K, n * K), pl.ds(t0 * T, nt_ * T)
            return xhi[r, lanes], xlo[r, lanes]

        def put(rb, cb, r, cl, v):
            g[SLOT[rb, cb, r, cl]] = v

        pairs, ys, zsum = {}, {}, {}

        def pair_start(s):
            span = pl.ds(*SPANS[s])
            pairs[s] = remote(g.at[span, pl.ds(at((1 - c) * 64), 64)], gr.at[span], gsend.at[s], grecv.at[s], dev(dc=1))
            start(pairs[s])

        def pair_finish(s):
            arrive(pairs[s])
            span = pl.ds(*SPANS[s])
            keep = pl.ds(at(c * 64), 64)
            g[span, keep, :] += gr[span]
            for d in (2, 1, 3):
                there = pl.ds(at(c * 64 + ((y + d) % 4) * 16), 16)
                ys[s, d] = remote(g.at[span, there], yr.at[d - 1, span], ysend.at[d - 1, s], yrecv.at[d - 1, s], dev(dy=d))
                start(ys[s, d])

        def y_finish(s):
            for d in (1, 3, 2):
                arrive(ys[s, d])
            first, n = SPANS[s]
            span = pl.ds(first, n)
            v = g[span, pl.ds(at(c * 64 + y * 16), 16), :] + yr[0, span] + yr[1, span] + yr[2, span]
            ybuf[pl.ds(first * 16, n * 16), :] = v.reshape(n * 16, T)
            if s not in GSPANS:
                return
            g0, ng = GSPANS[s]
            for group in range(g0, g0 + ng):
                for zz in range(8):
                    zs[zz, group] = ybuf[pl.ds(group * 64 + zz, 8, stride=8), :]
            for d in (4, 3, 5, 2, 6, 1, 7):
                zsum[s, d] = remote(
                    zs.at[(z + d) % 8, pl.ds(g0, ng)], zr.at[d - 1, pl.ds(g0, ng)],
                    zsend.at[d - 1, s], zrecv.at[d - 1, s], dev(dz=d),
                )
                start(zsum[s, d])

        def z_finish(s):
            for d in range(1, 8):
                arrive(zsum[s, d])
            span = pl.ds(*GSPANS[s])
            v = zs[z, span]
            for d in range(7):
                v = v + zr[d, span]
            f[pl.ds(GSPANS[s][0] * 8, GSPANS[s][1] * 8), :] = v.reshape(GSPANS[s][1] * 8, T)

        ybuf[pl.ds(63 * 16, 16), :] = jnp.zeros((16, T), F32)
        v = gram(own(0, 4), own(0, 4))
        for r in range(3):
            for q in range(3):
                put(0, 0, r, q, v[r * T : (r + 1) * T, q * T : (q + 1) * T])
        pair_start(0)
        pair_finish(0)

        extra_k = pl.ds(pl.multiple_of(jnp.where(c == 1, 2 * K, 3 * K), 16), K)

        def take(t, ks):
            for k in ks:
                traded(t, k).wait_recv()
                operand(xr[k, t], k, t, xhi, xlo)

        def cross(d, t, v):
            for q in range(3):
                w = v[:, q * T : (q + 1) * T]
                put(d, 0, t, q, w)
                put(0, d, q, t, w.T)

        def far(d, t, v):
            for q in range(v.shape[1] // T):
                w = v[:, q * T : (q + 1) * T]
                put(d, -d, t, q, w)
                put(-d, d, q, t, w.T)

        def whole(t, between=None):
            take(t, (1,))
            v2 = gram(got(1, 1, t, 1), own(1, 1))
            if between is not None:
                between()
            take(t, (2, 3))
            v1 = gram(got(2, 2, t, 1), own(0, 2))
            far_part(t)
            take(t, (4,))
            ve = gram(got(4, 1, t, 1), (ohi[extra_k, :], olo[extra_k, :]))
            cross(-1, t, v2 + jnp.where(c == 1, ve, 0.0))
            cross(1, t, v1 + jnp.where(c == 0, ve, 0.0))

        def left_part(t):
            take(t, (1, 4))
            ve = gram(got(4, 1, t, 1), (ohi[extra_k, :], olo[extra_k, :]))
            v2 = gram(got(1, 1, t, 1), own(1, 1))
            cross(-1, t, v2 + jnp.where(c == 1, ve, 0.0))
            return jnp.where(c == 0, ve, 0.0)

        def right_part(t, ve):
            take(t, (2, 3))
            cross(1, t, gram(got(2, 2, t, 1), own(0, 2)) + ve)

        def far_part(t):
            take(t, (0,))
            far(-1, t, gram(got(0, 2, t, 1), got(2, 2, 0, t + 1)))
            if t > 0:
                far(1, t, gram(got(2, 2, t, 1), got(0, 2, 0, t)))

        sent(0, "right1")
        send(1, "right1", "left1")
        send(1, 4)

        whole(0)
        pair_start(1)
        sent(1, "right1")
        send(2, 1, 2)
        send(2, 4)
        pair_finish(1)
        y_finish(0)

        whole(1, lambda: send(2, 0, 3))
        pair_start(2)
        z_finish(0)
        pair_finish(2)

        ve = left_part(2)
        pair_start(3)
        y_finish(1)
        pair_finish(3)
        right_part(2, ve)
        far_part(2)
        pair_start(4)
        z_finish(1)
        pair_finish(4)
        y_finish(2)
        y_finish(3)
        drain()
        y_finish(4)
        z_finish(2)
        z_finish(4)

        def strip(rb, cb, r):
            return jnp.concatenate([f[pl.ds(SLOT[rb, cb, r, q] * 2, 2), :] for q in range(3)], axis=1)

        def block(rb, cb):
            return jnp.concatenate([strip(rb, cb, r) for r in range(3)] + [jnp.zeros((2, NB), F32)], axis=0)

        def ordered(v):
            hi = v.astype(BF16)
            rest = v - hi.astype(F32)
            mid = rest.astype(BF16)
            low = (rest - mid.astype(F32)).astype(BF16)
            w = jnp.concatenate([hi.astype(F32), mid.astype(F32), low.astype(F32)], axis=0).astype(BF16)
            w = jnp.dot(w, onehot[...], preferred_element_type=F32)
            n = v.shape[0]
            return w[:n] + w[n : 2 * n] + w[2 * n :]

        for k, (rb, cb) in enumerate(((1, 0), (1, -1), (-1, 0), (-1, 1))):
            fs[k] = block(rb, cb)
        x_copies = [
            remote(fs.at[pl.ds(2 * k, 2)], fr.at[pl.ds(2 * k, 2)], xsend.at[k], xrecv.at[k], dev(dx=d))
            for k, d in ((0, 1), (1, 3))
        ]
        for copy in x_copies:
            start(copy)

        def lanes(d):
            return pl.ds(pl.multiple_of(((x + d) % 4) * NB, 128), NB)

        last = started[-2:]
        del started[-2:]
        drain()
        started.extend(last)
        o_ref[:, lanes(0)] = ordered(block(0, 0))[:6]
        right_, left_ = block(0, 1), block(0, -1)
        for copy in x_copies:
            arrive(copy)
        v = ordered(jnp.concatenate([right_ + fr[2], fr[1] + fr[3], left_ + fr[0]], axis=0))
        for d in range(3):
            o_ref[:, lanes(d + 1)] = v[8 * d : 8 * d + 6]

    work()
    drain()


def per_device(integrals, orbitals):
    dma = pltpu.SemaphoreType.DMA
    return pl.pallas_call(
        kernel,
        out_shape=jax.ShapeDtypeStruct((6, NL), F32),
        in_specs=[pl.BlockSpec(memory_space=pltpu.VMEM), pl.BlockSpec(memory_space=pl.ANY)],
        out_specs=pl.BlockSpec(memory_space=pltpu.VMEM),
        scratch_shapes=[
            pltpu.VMEM((NP, 12, NB, T), F32),
            pltpu.VMEM((3, NB, NL), BF16),
            pltpu.VMEM((3, NB, NL), BF16),
            pltpu.VMEM((4, 4 * SL, NB), F32),
            pltpu.VMEM((4 * SL, NL), BF16),
            pltpu.VMEM((4 * SL, NL), BF16),
            pltpu.VMEM((3, 4 * SL, NB), F32),
            pltpu.VMEM((5, 3, SL, NB), F32),
            pltpu.VMEM((4 * K, NB), BF16),
            pltpu.VMEM((4 * K, NB), BF16),
            pltpu.VMEM((5 * K, NB), BF16),
            pltpu.VMEM((5 * K, NB), BF16),
            pltpu.VMEM((63, T, T), F32),
            pltpu.VMEM((63, T // 2, T), F32),
            pltpu.VMEM((3, 63, 16, T), F32),
            pltpu.VMEM((1024, T), F32),
            pltpu.VMEM((8, 16, 8, T), F32),
            pltpu.VMEM((7, 16, 8, T), F32),
            pltpu.VMEM((128, T), F32),
            pltpu.VMEM((4, 8, NB), F32),
            pltpu.VMEM((4, 8, NB), F32),
            pltpu.VMEM((NB, NB), BF16),
            pltpu.SemaphoreType.REGULAR((5,)),
            dma((NP, 12)),
            dma((2, 3)), dma((2, 3)), dma((2, 3)), dma((2, 3)),
            dma((5, 3)), dma((5, 3)),
            dma((5,)), dma((5,)),
            dma((3, 5)), dma((3, 5)),
            dma((7, 5)), dma((7, 5)),
            dma((2,)), dma((2,)),
        ],
        compiler_params=pltpu.CompilerParams(
            collective_id=0, has_side_effects=True, vmem_limit_bytes=56 << 20
        ),
    )(orbitals.T, integrals)


def solution(mesh):
    return jax.shard_map(
        per_device,
        mesh=mesh,
        in_specs=(P("aux", "blk", None), P("blk", None)),
        out_specs=P(("blk", "aux"), None),
        check_vma=False,
    )
```
